32 devices in a mesh: dp: 1, expert: 32 (over z, y, x, core).
Axes of the slice: x: 2, y: 2, z: 4, core: 2. Of those that a mesh axis runs over, the one named last changes fastest.
Arguments:
- queries: bfloat16 [1024, 4096], P('dp', 'expert'), may hold values from -140 to 140
- keys: bfloat16 [1024, 256], P(('dp', 'expert')), may hold values from -4 to 4
- values: bfloat16 [1024, 256], P(('dp', 'expert')), may hold values from -4 to 4
- span_ids: int32 [1024], P('dp'), may hold values from 0 to 9, as said below
- residual: bfloat16 [1024, 4096], P(('dp', 'expert')), may hold values from -6 to 6
- norm_gain: float32 [4096], replicated, may hold values from 0.1 to 1.9
- routes: int32 [1024, 8], P(('dp', 'expert')), may hold values from 0 to 127, as said below
- gates: float32 [1024, 8], P(('dp', 'expert')), may hold values from 0.2 to 1
- w_gate: bfloat16 [4096, 4096], P('expert'), may hold values from -0.09375 to 0.09375
- w_up: bfloat16 [4096, 4096], P('expert'), may hold values from -0.09375 to 0.09375
- w_down: bfloat16 [4096, 4096], P('expert'), may hold values from -0.1875 to 0.1875
Outputs:
- mixed: bfloat16 [1024, 4096], P(('dp', 'expert'))
The draws below stay inside these ranges and needn't reach their ends.
Inputs may be any that keep to these rules, and one draw needn't show every extreme that they name: `span_ids`: span numbers start at 0 and never fall along the positions; every span starts at an even position, has 2 to 512 positions and never crosses a multiple of 512; one aligned block of 512 positions is a single span, and every other holds exactly 9 spans. `routes`: each row names 8 different experts. In the rows of one device (aligned blocks of 32 rows) each expert below 4 is named by at most 8 rows, and exactly one such expert, changing from block to block, by exactly 8 rows; every expert below 4 is that one in some block.
All inputs are finite; a program needn't handle non-finite values.
Results may differ from the reference program's by a relative error of at most 0.0054.
Values may be sent and summed in bfloat16 or wider, within the bound.
A program may use at most 64 MiB of HBM per device.

```python
import math
import jax
import jax.numpy as jnp
from jax import lax

D = 4096
HEADS = 64
KV_HEADS = 4
EXPERTS = 128
TOP = 8
HEAD_DIM = 64
FF_WIN = 1024
FF_DEV = 128
SPAN = 512
TOK_DEV = 32
TOKENS = 1024
WAVE = 4


def shared_keys(key):
    sampled = jax.random.normal(jax.random.fold_in(key, 101), (TOKENS, KV_HEADS * HEAD_DIM), jnp.float32)
    return jnp.clip(sampled, -4.0, 4.0)


def draw_keys(key, part):
    key_rows = shared_keys(key)
    return key_rows.astype(jnp.bfloat16)


def draw_queries(key, part):
    sampled = jnp.clip(jax.random.normal(jax.random.fold_in(key, 102), (TOKENS, D), jnp.float32), -4.0, 4.0)
    return sampled.astype(jnp.bfloat16)


def draw_span_ids(key, part):
    blocks = TOKENS // SPAN
    pairs = SPAN // 2
    extra = SPAN // 64
    whole_block = jax.random.randint(jax.random.fold_in(key, 301), (), 0, blocks)
    scores = jax.random.randint(jax.random.fold_in(key, 302), (blocks, pairs), 0, 1 << 20) * pairs + jnp.arange(pairs)[None, :]
    scores = jnp.where(jnp.arange(pairs)[None, :] == 0, 1 << 30, scores)
    rank_order = jnp.argsort(jnp.argsort(scores, axis=1), axis=1)
    cut_pair = rank_order < extra
    cut_pair = cut_pair & (jnp.arange(blocks)[:, None] != whole_block)
    first_pair = jnp.arange(pairs)[None, :] == 0
    starts_pair = cut_pair | first_pair
    starts = jnp.stack([starts_pair, jnp.zeros_like(starts_pair)], axis=2).reshape(TOKENS)
    return (jnp.cumsum(starts.astype(jnp.int32)) - 1).astype(jnp.int32)


def draw_routes(key, part):
    blocks = TOKENS // TOK_DEV
    capacity = TOK_DEV // 4
    spare_ids = EXPERTS - WAVE
    base = jax.random.randint(jax.random.fold_in(key, 201), (), 0, WAVE)
    favored = (base + jnp.arange(blocks)) % WAVE
    modest = jax.random.randint(jax.random.fold_in(key, 202), (blocks, WAVE), 1, capacity // 2 + 1)
    counts = jnp.where(jnp.arange(WAVE)[None, :] == favored[:, None], capacity, modest)
    scores = jax.random.randint(jax.random.fold_in(key, 203), (blocks, WAVE, TOK_DEV), 0, 1 << 20) * TOK_DEV + jnp.arange(TOK_DEV)
    rank_order = jnp.argsort(jnp.argsort(scores, axis=2), axis=2)
    chosen = rank_order < counts[:, :, None]
    chosen = jnp.transpose(chosen, (0, 2, 1)).reshape(TOKENS, WAVE)
    taken_count = jnp.sum(chosen.astype(jnp.int32), axis=1)
    position = jnp.cumsum(chosen.astype(jnp.int32), axis=1) - 1
    columns = jnp.arange(TOP)
    matches = chosen[:, :, None] & (position[:, :, None] == columns[None, None, :])
    inside = jnp.sum(jnp.where(matches, jnp.arange(WAVE)[None, :, None], 0), axis=1)
    offset = jax.random.randint(jax.random.fold_in(key, 204), (TOKENS,), 0, spare_ids)
    outside = WAVE + (offset[:, None] + columns[None, :] - taken_count[:, None]) % spare_ids
    listed = jnp.where(columns[None, :] < taken_count[:, None], inside, outside)
    shuffle = jax.random.randint(jax.random.fold_in(key, 205), (TOKENS, TOP), 0, 1 << 20) * TOP + columns[None, :]
    reorder = jnp.argsort(shuffle, axis=1)
    return jnp.take_along_axis(listed, reorder, axis=1).astype(jnp.int32)


def levels(key, shape, cuts, smallest, high):
    def one(axis_at, parts):
        heights = jax.random.uniform(jax.random.fold_in(jax.random.fold_in(key, 6), axis_at), (parts,), jnp.float32, smallest / len(cuts), high / len(cuts))
        return jnp.repeat(jnp.exp(heights), shape[axis_at] // parts).reshape((-1,) + (1,) * (len(shape) - axis_at - 1))

    factor_of = one(*cuts[0])
    for cut in cuts[1:]:
        factor_of = factor_of * one(*cut)
    return factor_of


def noise(key, extent, scale, reach, shards=(), held_as=jnp.bfloat16):
    result = scale * jax.random.normal(key, extent, jnp.float32)
    if shards:
        result = result * levels(key, extent, shards, -0.22, 0.18)
    return jnp.clip(result, -reach, reach).astype(held_as)


def setup_inputs(seed: int = 0, part: int = 0) -> dict:
    arg_keys = jax.random.split(jax.random.key(seed), 12)
    part_splits = jax.random.split(jax.random.fold_in(arg_keys[11], part), 12)
    return {
        "queries": draw_queries(jax.random.fold_in(jax.random.fold_in(arg_keys[11], part), 71), part),
        "keys": draw_keys(jax.random.fold_in(jax.random.fold_in(arg_keys[11], part), 71), part),
        "values": noise(part_splits[2], (TOKENS, KV_HEADS * HEAD_DIM), 1.0, 4.0, ((0, 32),)),
        "span_ids": draw_span_ids(jax.random.fold_in(jax.random.fold_in(arg_keys[11], part), 71), part),
        "residual": noise(part_splits[4], (TOKENS, D), 1.0, 6.0, ((0, 32),)),
        "norm_gain": jnp.clip(1.0 + 0.18 * jax.random.normal(arg_keys[5], (D,), jnp.float32), 0.1, 1.9),
        "routes": draw_routes(jax.random.fold_in(jax.random.fold_in(arg_keys[11], part), 71), part),
        "gates": jnp.clip(0.2 + 0.8 * jax.random.uniform(part_splits[7], (TOKENS, TOP), jnp.float32) ** levels(part_splits[7], (TOKENS, TOP), ((0, 32),), -0.2, 0.2), 0.2, 1.0),
        "w_gate": noise(arg_keys[8], (WAVE * FF_WIN, D), D ** -0.5, 0.09375, ((0, 32),)),
        "w_up": noise(arg_keys[9], (WAVE * FF_WIN, D), D ** -0.5, 0.09375, ((0, 32),)),
        "w_down": noise(arg_keys[10], (WAVE * FF_WIN, D), FF_WIN ** -0.5, 0.1875, ((0, 32),)),
    }


def reference(queries, keys, values, span_ids, residual, norm_gain, routes, gates, w_gate, w_up, w_down):
    group_heads = HEADS // KV_HEADS
    blocks = TOKENS // SPAN
    score_scale = 1.0 / math.sqrt(HEAD_DIM)
    positions = jnp.arange(SPAN)
    causal = positions[None, :] <= positions[:, None]

    def one_block(pieces):
        query_blk, key_blk, value_blk, ids_blk = pieces
        key_full = jnp.repeat(key_blk, group_heads, axis=1).astype(jnp.float32)
        value_full = jnp.repeat(value_blk, group_heads, axis=1).astype(jnp.float32)
        scores = jnp.einsum('qhd,khd->hqk', query_blk.astype(jnp.float32), key_full) * score_scale
        allowed = causal & (ids_blk[None, :] == ids_blk[:, None])
        scores = jnp.where(allowed[None], scores, -jnp.inf)
        highest = lax.optimization_barrier(jnp.max(scores, axis=-1, keepdims=True))
        raised = jnp.exp(scores - highest)
        probabilities = raised / lax.optimization_barrier(jnp.sum(raised, axis=-1, keepdims=True))
        attn_weights = lax.optimization_barrier(probabilities.astype(jnp.bfloat16))
        attended_blk = jnp.einsum('hqk,khd->qhd', attn_weights.astype(jnp.float32), value_full)
        return attended_blk.astype(jnp.bfloat16)
    attended = lax.map(one_block, (queries.reshape(blocks, SPAN, HEADS, HEAD_DIM), keys.reshape(blocks, SPAN, KV_HEADS, HEAD_DIM), values.reshape(blocks, SPAN, KV_HEADS, HEAD_DIM), span_ids.reshape(blocks, SPAN))).reshape(TOKENS, D)
    stream = (residual.astype(jnp.float32) + attended.astype(jnp.float32)).astype(jnp.bfloat16)
    stream_wide = stream.astype(jnp.float32)
    inverse = lax.rsqrt(lax.optimization_barrier(jnp.mean(stream_wide * stream_wide, axis=-1, keepdims=True)) + 1e-06)
    normed = (stream_wide * inverse * norm_gain.astype(jnp.float32)).astype(jnp.bfloat16)
    group = FF_WIN // FF_DEV
    most_rows = TOKENS // 4

    def one_expert(total, expert):
        hits = routes == expert
        named = jnp.any(hits, axis=1)
        weight = lax.optimization_barrier(jnp.sum(jnp.where(hits, gates, 0.0), axis=1))
        number = jnp.sum(named.astype(jnp.int32))
        index = jnp.nonzero(named, size=most_rows, fill_value=0)[0].astype(jnp.int32)
        valid = jnp.arange(most_rows, dtype=jnp.int32) < number
        token_rows = normed[index]
        start = (expert * FF_WIN).astype(jnp.int32)
        gate_rows = lax.dynamic_slice_in_dim(w_gate, start, FF_WIN, 0)
        up_rows = lax.dynamic_slice_in_dim(w_up, start, FF_WIN, 0)
        down_rows = lax.dynamic_slice_in_dim(w_down, start, FF_WIN, 0)
        dims = (((1,), (1,)), ((), ()))
        gate_pre = lax.dot_general(token_rows, gate_rows, dims, preferred_element_type=jnp.float32)
        up_pre = lax.dot_general(token_rows, up_rows, dims, preferred_element_type=jnp.float32)
        hidden = lax.optimization_barrier((jax.nn.silu(gate_pre) * up_pre).astype(jnp.bfloat16))
        partial_sums = jnp.einsum('rgf,gfd->grd', hidden.reshape(most_rows, group, FF_DEV).astype(jnp.float32), down_rows.reshape(group, FF_DEV, D).astype(jnp.float32))
        rounded = lax.optimization_barrier(partial_sums.astype(jnp.bfloat16))
        expert_out = lax.optimization_barrier(jnp.sum(rounded.astype(jnp.float32), axis=0))
        contribution = jnp.where(valid, weight[index], 0.0)[:, None] * expert_out
        return (total.at[index].add(contribution), None)
    total, _ = lax.scan(one_expert, jnp.zeros((TOKENS, D), jnp.float32), jnp.arange(WAVE, dtype=jnp.int32))
    return (stream_wide + total).astype(jnp.bfloat16)
```

```python
import math

import jax
import jax.numpy as jnp
from jax import lax
from jax.sharding import PartitionSpec as P

KV_HEADS = 4
HEAD_DIM = 64
FF_WIN = 1024
SPAN = 512


def from_partner(value, axis, distance):
    mask = 2**distance
    pairs = [(source, source ^ mask) for source in range(lax.axis_size(axis))]
    return lax.ppermute(value, axis, pairs)


def attend(queries, key_mine, value_mine, span_ids):
    tokens_all, head_width = queries.shape
    heads_here = head_width // HEAD_DIM
    blocks = tokens_all // SPAN
    score_scale = 1.0 / math.sqrt(HEAD_DIM)
    positions = jnp.arange(SPAN)
    causal = positions[None, :] <= positions[:, None]

    def one_block(pieces):
        query_blk, key_blk, value_blk, ids_blk = pieces
        scores = (
            jnp.einsum("qhd,kd->hqk", query_blk, key_blk, preferred_element_type=jnp.float32)
            * score_scale
        )
        allowed = causal & (ids_blk[None, :] == ids_blk[:, None])
        scores = jnp.where(allowed[None], scores, -jnp.inf)
        highest = jnp.max(scores, axis=-1, keepdims=True)
        raised = jnp.exp(scores - highest)
        attn_weights = (raised / jnp.sum(raised, axis=-1, keepdims=True)).astype(jnp.bfloat16)
        attended_blk = jnp.einsum(
            "hqk,kd->qhd", attn_weights, value_blk, preferred_element_type=jnp.float32
        )
        return attended_blk.astype(jnp.bfloat16)

    result = lax.map(
        one_block,
        (
            queries.reshape(blocks, SPAN, heads_here, HEAD_DIM),
            key_mine.reshape(blocks, SPAN, HEAD_DIM),
            value_mine.reshape(blocks, SPAN, HEAD_DIM),
            span_ids.reshape(blocks, SPAN),
        ),
    )
    return result.reshape(tokens_all, head_width)


def shards(
    queries, keys, values, span_ids, residual, norm_gain, routes, gates, w_gate, w_up, w_down
):
    devices = lax.axis_size("expert")
    my_index = lax.axis_index("expert")
    tok_local = residual.shape[0]
    joined = jnp.concatenate(
        [
            keys.reshape(tok_local, KV_HEADS, HEAD_DIM),
            values.reshape(tok_local, KV_HEADS, HEAD_DIM),
        ],
        axis=2,
    )
    spread = jnp.repeat(joined, devices // KV_HEADS, axis=1)
    arrived_heads = lax.all_to_all(spread, "expert", split_axis=1, concat_axis=0, tiled=True)
    key_mine = arrived_heads[:, 0, :HEAD_DIM]
    value_mine = arrived_heads[:, 0, HEAD_DIM:]
    attended_heads = attend(queries, key_mine, value_mine, span_ids)
    attended = lax.all_to_all(attended_heads, "expert", split_axis=0, concat_axis=1, tiled=True)
    stream_wide = residual.astype(jnp.float32) + attended.astype(jnp.float32)
    stream = stream_wide.astype(jnp.bfloat16)
    stream_wide = stream.astype(jnp.float32)
    inverse = lax.rsqrt(jnp.mean(stream_wide * stream_wide, axis=-1, keepdims=True) + 1e-06)
    normed = (stream_wide * inverse * norm_gain).astype(jnp.bfloat16)
    group = FF_WIN // w_gate.shape[0]
    group_bits = group.bit_length() - 1
    wave = devices // group
    capacity = tok_local // 4
    slot_count = capacity // group
    model_width = normed.shape[1]
    expert_ids = jnp.arange(wave, dtype=jnp.int32)
    hits = routes[:, :, None] == expert_ids[None, None, :]
    named = jnp.any(hits, axis=1)
    weight = jnp.sum(jnp.where(hits, gates[:, :, None], 0.0), axis=1)
    ahead = jnp.arange(tok_local)[None, :, None] <= jnp.arange(tok_local)[:, None, None]
    slot_index = jnp.sum((ahead & named[None, :, :]).astype(jnp.int32), axis=1) - 1
    selector = named.T[:, None, :] & (
        slot_index.T[:, None, :] == jnp.arange(capacity)[None, :, None]
    )
    outgoing = jnp.einsum(
        "ect,td->ecd", selector.astype(jnp.bfloat16), normed, preferred_element_type=jnp.float32
    ).astype(jnp.bfloat16)
    outgoing = outgoing.reshape(devices, slot_count, model_width)
    gathered = lax.all_to_all(outgoing, "expert", split_axis=0, concat_axis=0, tiled=True)
    for bit_number in range(group_bits):
        partner = from_partner(gathered, "expert", bit_number)
        lower = my_index // 2**bit_number % 2 == 0
        gathered = jnp.where(
            lower,
            jnp.concatenate([gathered, partner], axis=1),
            jnp.concatenate([partner, gathered], axis=1),
        )
    token_rows = gathered.reshape(devices * capacity, model_width)
    dims = (((1,), (1,)), ((), ()))
    gate_pre = lax.dot_general(token_rows, w_gate, dims, preferred_element_type=jnp.float32)
    up_pre = lax.dot_general(token_rows, w_up, dims, preferred_element_type=jnp.float32)
    hidden = (jax.nn.silu(gate_pre) * up_pre).astype(jnp.bfloat16)
    piece = jnp.dot(hidden, w_down, preferred_element_type=jnp.float32).astype(jnp.bfloat16)
    piece = piece.reshape(devices, capacity, model_width)
    returned = lax.all_to_all(piece, "expert", split_axis=0, concat_axis=0, tiled=True)
    expert_out = jnp.sum(
        returned.reshape(wave, group, capacity, model_width).astype(jnp.float32), axis=1
    )
    flat_slots = expert_ids[None, :] * capacity + jnp.maximum(slot_index, 0)
    picked = jnp.take(
        expert_out.reshape(wave * capacity, model_width), flat_slots.reshape(-1), axis=0
    )
    picked = picked.reshape(tok_local, wave, model_width)
    combined = jnp.sum(weight[:, :, None] * picked, axis=1)
    return (stream_wide + combined).astype(jnp.bfloat16)


def solution(mesh):
    return jax.shard_map(
        shards,
        mesh=mesh,
        in_specs=(
            P("dp", "expert"),
            P(("dp", "expert"), None),
            P(("dp", "expert"), None),
            P("dp"),
            P(("dp", "expert"), None),
            P(),
            P(("dp", "expert"), None),
            P(("dp", "expert"), None),
            P("expert", None),
            P("expert", None),
            P("expert", None),
        ),
        out_specs=P(("dp", "expert"), None),
        check_vma=False,
    )
```

```python
import functools
import math

import jax
import jax.numpy as jnp
from jax import lax
from jax.experimental import pallas as pl
from jax.experimental.pallas import tpu as pltpu
from jax.sharding import PartitionSpec as P

KV_HEADS = 4
HEAD_DIM = 64
FF_WIN = 1024
SPAN = 512
MESH = pl.DeviceIdType.MESH
F32 = jnp.float32
BF16 = jnp.bfloat16


def remote(src, dst, send, recv, device):
    return pltpu.make_async_remote_copy(
        src_ref=src, dst_ref=dst, send_sem=send, recv_sem=recv,
        device_id={"expert": device}, device_id_type=MESH,
    )


def route_matrix(routes, gates, wave, capacity):
    tokens = routes.shape[0]
    columns = wave * capacity
    column = lax.broadcasted_iota(jnp.int32, (tokens, columns), 1)
    lower = (
        lax.broadcasted_iota(jnp.int32, (tokens, tokens), 0)
        >= lax.broadcasted_iota(jnp.int32, (tokens, tokens), 1)
    ).astype(F32)
    named_wide = jnp.zeros((tokens, columns), F32)
    weight_wide = jnp.zeros((tokens, columns), F32)
    for expert in range(wave):
        hits = routes == expert
        named = jnp.max(jnp.where(hits, 1.0, 0.0), axis=1, keepdims=True)
        weight = jnp.sum(jnp.where(hits, gates, 0.0), axis=1, keepdims=True)
        here = column // capacity == expert
        named_wide = jnp.where(here, named, named_wide)
        weight_wide = jnp.where(here, weight, weight_wide)
    count = jnp.dot(lower.astype(BF16), named_wide.astype(BF16), preferred_element_type=F32)
    slot = (column % capacity + 1).astype(F32)
    chosen = jnp.where(count == slot, named_wide, 0.0)
    return chosen, chosen * weight_wide


def moe_kernel(
    group, att, res, gain, routes, gates, wg, wu, wd, out,
    wgu_v, wd_v, outg, x_buf, part, core_buf, sums, plane_buf, final, back,
    w_sem, z_send, x_send, x_recv, c_send, c_recv, p_send, p_recv, b_send, b_recv,
):
    me = lax.axis_index("expert")
    wave = outg.shape[0]
    capacity = outg.shape[1] // 2
    tokens, width = res.shape
    half = width // 2
    hidden_here = wg.shape[0]
    mine = me % group
    plane = me // group
    base = plane * group

    def across(rz):
        return (plane ^ rz) * group + mine

    def within(r):
        return base + (mine ^ r)

    weights = [
        pltpu.make_async_copy(wg, wgu_v.at[pl.ds(0, hidden_here)], w_sem.at[0]),
        pltpu.make_async_copy(wu, wgu_v.at[pl.ds(hidden_here, hidden_here)], w_sem.at[1]),
        pltpu.make_async_copy(wd, wd_v, w_sem.at[2]),
    ]
    for copy in weights:
        copy.start()
    barrier = pltpu.get_barrier_semaphore()
    partners = [across(rz) for rz in range(1, wave)] + [within(r) for r in (1, 2, 4, 6)]
    for device in partners:
        pl.semaphore_signal(barrier, inc=1, device_id={"expert": device}, device_id_type=MESH)

    chosen, mix = route_matrix(routes[...], gates[...], wave, capacity)
    stream = (res[...].astype(F32) + att[...].astype(F32)).astype(BF16).astype(F32)
    inverse = lax.rsqrt(jnp.mean(stream * stream, axis=-1, keepdims=True) + 1e-06)
    normed = (stream * inverse * gain[...]).astype(BF16)
    rows = jnp.dot(chosen.T.astype(BF16), normed, preferred_element_type=F32)
    for expert in range(wave):
        block = rows[expert * capacity:(expert + 1) * capacity]
        outg[expert] = jnp.concatenate([block[:, :half], block[:, half:]], axis=0).astype(BF16)
    pl.semaphore_wait(barrier, len(partners))

    sends = []

    def go(copy):
        copy.start()
        sends.append(copy)
        return copy

    def arrived(ref, sem):
        pltpu.make_async_copy(ref, ref, sem).wait()

    for rz in range(1, wave):
        go(remote(outg.at[plane ^ rz], x_buf.at[0, rz], z_send.at[rz], x_recv.at[0, rz], across(rz)))
    x_buf[0, 0] = outg[plane]
    for rz in range(wave):
        if rz:
            arrived(x_buf.at[0, rz], x_recv.at[0, rz])
        for r in (2, 4, 6, 1):
            go(remote(x_buf.at[0, rz], x_buf.at[r, rz], x_send.at[r, rz], x_recv.at[r, rz], within(r)))
    for copy in weights:
        copy.wait()

    def fold(k):
        arrived(core_buf.at[k], c_recv.at[k])
        total = part[2 * k].astype(F32) + core_buf[k].astype(F32)
        sums[k] = total.astype(BF16)
        if k:
            go(remote(sums.at[k], plane_buf.at[k], p_send.at[k], p_recv.at[k], within(2 * k)))

    dims = (((1,), (1,)), ((), ()))
    pairs = group // 2
    for k in range(pairs):
        r = 2 * k
        if k:
            for rz in range(wave):
                arrived(x_buf.at[r, rz], x_recv.at[r, rz])
                go(remote(x_buf.at[r, rz], x_buf.at[r + 1, rz], x_send.at[r + 1, rz],
                          x_recv.at[r + 1, rz], within(1)))
        for rz in range(wave):
            arrived(x_buf.at[r + 1, rz], x_recv.at[r + 1, rz])
        x = x_buf[r:r + 2].reshape(2 * wave * 2 * capacity, half)
        left = lax.dot_general(x, wgu_v[:, :half], dims, preferred_element_type=F32)
        right = lax.dot_general(x, wgu_v[:, half:], dims, preferred_element_type=F32)
        left = left.reshape(2 * wave, 2 * capacity, 2 * hidden_here)[:, :capacity]
        right = right.reshape(2 * wave, 2 * capacity, 2 * hidden_here)[:, capacity:]
        pre = (left + right).reshape(2 * wave * capacity, 2 * hidden_here)
        gate_pre, up_pre = pre[:, :hidden_here], pre[:, hidden_here:]
        hidden = (gate_pre / (1.0 + jnp.exp(-gate_pre)) * up_pre).astype(BF16)
        piece = jnp.dot(hidden, wd_v[...], preferred_element_type=F32).astype(BF16)
        part[r] = piece[:wave * capacity]
        part[r + 1] = piece[wave * capacity:]
        go(remote(part.at[r + 1], core_buf.at[k], c_send.at[k], c_recv.at[k], within(1)))
        if k:
            fold(k - 1)
    fold(pairs - 1)

    total = sums[0].astype(F32)
    for k in range(1, pairs):
        arrived(plane_buf.at[k], p_recv.at[k])
        total = total + plane_buf[k].astype(F32)
    for rz in range(wave):
        block = total[rz * capacity:(rz + 1) * capacity]
        block = jnp.concatenate([block[:, :half], block[:, half:]], axis=0).astype(BF16)
        if rz:
            final[rz] = block
            go(remote(final.at[rz], back.at[plane], b_send.at[rz], b_recv.at[rz], across(rz)))
        else:
            back[plane] = block
    for rz in range(1, wave):
        arrived(back.at[plane ^ rz], b_recv.at[rz])

    high = mix.astype(BF16)
    rest = mix - high.astype(F32)
    middle = rest.astype(BF16)
    low = (rest - middle.astype(F32)).astype(BF16)
    outs = back[...].astype(F32)
    for side in range(2):
        columns = slice(side * half, (side + 1) * half)
        block = outs[:, side * capacity:(side + 1) * capacity].reshape(wave * capacity, half).astype(BF16)
        added = (
            jnp.dot(low, block, preferred_element_type=F32)
            + jnp.dot(middle, block, preferred_element_type=F32)
            + jnp.dot(high, block, preferred_element_type=F32)
        )
        out[:, columns] = (stream[:, columns] + added).astype(BF16)
    for copy in sends:
        copy.wait_send()


def experts(att, res, gain, routes, gates, wg, wu, wd):
    devices = lax.axis_size("expert")
    group = FF_WIN // wg.shape[0]
    wave = devices // group
    tokens, width = res.shape
    capacity = tokens // 4
    half = width // 2
    pairs = group // 2
    vmem = pl.BlockSpec(memory_space=pltpu.VMEM)
    hbm = pl.BlockSpec(memory_space=pl.ANY)
    dma = pltpu.SemaphoreType.DMA
    rows = wave * capacity
    return pl.pallas_call(
        functools.partial(moe_kernel, group),
        out_shape=jax.ShapeDtypeStruct((tokens, width), BF16),
        in_specs=[vmem] * 5 + [hbm] * 3,
        out_specs=vmem,
        scratch_shapes=[
            pltpu.VMEM((2 * wg.shape[0], width), BF16),
            pltpu.VMEM((wd.shape[0], width), BF16),
            pltpu.VMEM((wave, 2 * capacity, half), BF16),
            pltpu.VMEM((group, wave, 2 * capacity, half), BF16),
            pltpu.VMEM((group, rows, width), BF16),
            pltpu.VMEM((pairs, rows, width), BF16),
            pltpu.VMEM((pairs, rows, width), BF16),
            pltpu.VMEM((pairs, rows, width), BF16),
            pltpu.VMEM((wave, 2 * capacity, half), BF16),
            pltpu.VMEM((wave, 2 * capacity, half), BF16),
            dma((3,)), dma((wave,)), dma((group, wave)), dma((group, wave)),
            dma((pairs,)), dma((pairs,)), dma((pairs,)), dma((pairs,)), dma((wave,)), dma((wave,)),
        ],
        compiler_params=pltpu.CompilerParams(
            collective_id=0, has_side_effects=True, vmem_limit_bytes=48 * 2**20
        ),
    )(att, res, gain.reshape(1, width), routes, gates, wg, wu, wd)


def attend(queries, key_mine, value_mine, span_ids):
    tokens_all, head_width = queries.shape
    heads_here = head_width // HEAD_DIM
    blocks = tokens_all // SPAN
    score_scale = 1.0 / math.sqrt(HEAD_DIM)
    positions = jnp.arange(SPAN)
    causal = positions[None, :] <= positions[:, None]

    def one_block(pieces):
        query_blk, key_blk, value_blk, ids_blk = pieces
        scores = (
            jnp.einsum("qhd,kd->hqk", query_blk, key_blk, preferred_element_type=jnp.float32)
            * score_scale
        )
        allowed = causal & (ids_blk[None, :] == ids_blk[:, None])
        scores = jnp.where(allowed[None], scores, -jnp.inf)
        highest = jnp.max(scores, axis=-1, keepdims=True)
        raised = jnp.exp(scores - highest)
        attn_weights = (raised / jnp.sum(raised, axis=-1, keepdims=True)).astype(jnp.bfloat16)
        attended_blk = jnp.einsum(
            "hqk,kd->qhd", attn_weights, value_blk, preferred_element_type=jnp.float32
        )
        return attended_blk.astype(jnp.bfloat16)

    result = lax.map(
        one_block,
        (
            queries.reshape(blocks, SPAN, heads_here, HEAD_DIM),
            key_mine.reshape(blocks, SPAN, HEAD_DIM),
            value_mine.reshape(blocks, SPAN, HEAD_DIM),
            span_ids.reshape(blocks, SPAN),
        ),
    )
    return result.reshape(tokens_all, head_width)


def shards(
    queries, keys, values, span_ids, residual, norm_gain, routes, gates, w_gate, w_up, w_down
):
    devices = lax.axis_size("expert")
    tok_local = residual.shape[0]
    joined = jnp.concatenate(
        [
            keys.reshape(tok_local, KV_HEADS, HEAD_DIM),
            values.reshape(tok_local, KV_HEADS, HEAD_DIM),
        ],
        axis=2,
    )
    spread = jnp.repeat(joined, devices // KV_HEADS, axis=1)
    arrived_heads = lax.all_to_all(spread, "expert", split_axis=1, concat_axis=0, tiled=True)
    key_mine = arrived_heads[:, 0, :HEAD_DIM]
    value_mine = arrived_heads[:, 0, HEAD_DIM:]
    attended_heads = attend(queries, key_mine, value_mine, span_ids)
    attended = lax.all_to_all(attended_heads, "expert", split_axis=0, concat_axis=1, tiled=True)
    return experts(attended, residual, norm_gain, routes, gates, w_gate, w_up, w_down)


def solution(mesh):
    return jax.shard_map(
        shards,
        mesh=mesh,
        in_specs=(
            P("dp", "expert"),
            P(("dp", "expert"), None),
            P(("dp", "expert"), None),
            P("dp"),
            P(("dp", "expert"), None),
            P(),
            P(("dp", "expert"), None),
            P(("dp", "expert"), None),
            P("expert", None),
            P("expert", None),
            P("expert", None),
        ),
        out_specs=P(("dp", "expert"), None),
        check_vma=False,
    )
```

```python
import functools
import math

import jax
import jax.numpy as jnp
from jax import lax
from jax.experimental import pallas as pl
from jax.experimental.pallas import tpu as pltpu
from jax.sharding import PartitionSpec as P

KV_HEADS = 4
HEAD_DIM = 64
FF_WIN = 1024
SPAN = 512
MESH = pl.DeviceIdType.MESH
F32 = jnp.float32
BF16 = jnp.bfloat16


def remote(src, dst, send, recv, device):
    return pltpu.make_async_remote_copy(
        src_ref=src, dst_ref=dst, send_sem=send, recv_sem=recv,
        device_id={"expert": device}, device_id_type=MESH,
    )


def route_matrix(routes, gates, wave, capacity):
    tokens = routes.shape[0]
    columns = wave * capacity
    column = lax.broadcasted_iota(jnp.int32, (tokens, columns), 1)
    lower = (
        lax.broadcasted_iota(jnp.int32, (tokens, tokens), 0)
        >= lax.broadcasted_iota(jnp.int32, (tokens, tokens), 1)
    ).astype(F32)
    named_wide = jnp.zeros((tokens, columns), F32)
    weight_wide = jnp.zeros((tokens, columns), F32)
    for expert in range(wave):
        hits = routes == expert
        named = jnp.max(jnp.where(hits, 1.0, 0.0), axis=1, keepdims=True)
        weight = jnp.sum(jnp.where(hits, gates, 0.0), axis=1, keepdims=True)
        here = column // capacity == expert
        named_wide = jnp.where(here, named, named_wide)
        weight_wide = jnp.where(here, weight, weight_wide)
    count = jnp.dot(lower.astype(BF16), named_wide.astype(BF16), preferred_element_type=F32)
    slot = (column % capacity + 1).astype(F32)
    chosen = jnp.where(count == slot, named_wide, 0.0)
    return chosen, chosen * weight_wide


def moe_kernel(
    group, queries, keys, values, ids, res, gain, routes, gates, wg, wu, wd, out,
    kv_out, kv_buf, id_rows, att_in, att_own, att_buf,
    kz_send, kv_send, kv_recv, az_send, az_recv, a_send, a_recv,
    wgu_v, wd_v, outg, x_buf, part, core_buf, sums, plane_buf, final, back,
    w_sem, z_send, x_send, x_recv, c_send, c_recv, p_send, p_recv, b_send, b_recv,
):
    me = lax.axis_index("expert")
    wave = outg.shape[0]
    capacity = outg.shape[1] // 2
    tokens, width = res.shape
    half = width // 2
    hidden_here = wg.shape[0]
    mine = me % group
    plane = me // group
    base = plane * group

    def across(rz):
        return (plane ^ rz) * group + mine

    def within(r):
        return base + (mine ^ r)

    weights = [
        pltpu.make_async_copy(wg, wgu_v.at[pl.ds(0, hidden_here)], w_sem.at[0]),
        pltpu.make_async_copy(wu, wgu_v.at[pl.ds(hidden_here, hidden_here)], w_sem.at[1]),
        pltpu.make_async_copy(wd, wd_v, w_sem.at[2]),
    ]
    for copy in weights:
        copy.start()
    barrier = pltpu.get_barrier_semaphore()
    partners = [across(rz) for rz in range(1, wave)] + [within(r) for r in range(1, group)]
    for device in partners:
        pl.semaphore_signal(barrier, inc=1, device_id={"expert": device}, device_id_type=MESH)

    for plane_to in range(wave):
        head = plane_to * KV_HEADS // wave
        columns = slice(head * HEAD_DIM, (head + 1) * HEAD_DIM)
        kv_out[plane_to] = jnp.concatenate([keys[:, columns], values[:, columns]], axis=1)
    pl.semaphore_wait(barrier, len(partners))

    sends = []

    def go(copy):
        copy.start()
        sends.append(copy)
        return copy

    def arrived(ref, sem):
        pltpu.make_async_copy(ref, ref, sem).wait()

    for rz in range(1, wave):
        go(remote(kv_out.at[plane ^ rz], kv_buf.at[plane, mine], kz_send.at[rz], kv_recv.at[rz, 0], across(rz)))
    kv_buf[plane, mine] = kv_out[plane]
    for rz in range(wave):
        block = kv_buf.at[plane ^ rz, mine]
        if rz:
            arrived(block, kv_recv.at[rz, 0])
        for r in range(1, group):
            go(remote(block, block, kv_send.at[rz, r], kv_recv.at[rz, r], within(r)))

    chosen, mix = route_matrix(routes[...], gates[...], wave, capacity)
    chunk = group * tokens
    for index in range(wave):
        id_rows[index] = jnp.broadcast_to(ids[index].astype(F32), (128, chunk)).T
    for rz in range(wave):
        for r in range(1, group):
            arrived(kv_buf.at[plane ^ rz, mine ^ r], kv_recv.at[rz, r])

    def attend(index):
        planes = SPAN // chunk
        first = index // planes * planes
        block = kv_buf[pl.ds(first, planes)].reshape(SPAN, 2 * HEAD_DIM)
        key_blk = block[:, :HEAD_DIM]
        value_rows = block.T[HEAD_DIM:]
        key_ids = id_rows[pl.ds(first, planes)].reshape(SPAN, 128)
        key_ids = jnp.concatenate([key_ids] * (chunk // 128), axis=1)
        offset = (index - first) * chunk
        ahead = (
            lax.broadcasted_iota(jnp.int32, (SPAN, chunk), 0)
            - lax.broadcasted_iota(jnp.int32, (SPAN, chunk), 1)
        )
        allowed = (ahead <= offset) & (key_ids == ids[index].astype(F32))
        query = queries[pl.ds(pl.multiple_of(index * chunk, chunk), chunk), :] * BF16(1.0 / math.sqrt(HEAD_DIM))
        heads = []
        for head in range(query.shape[1] // HEAD_DIM):
            one = query[:, head * HEAD_DIM:(head + 1) * HEAD_DIM]
            scores = lax.dot_general(key_blk, one, (((1,), (1,)), ((), ())), preferred_element_type=F32)
            scores = jnp.where(allowed, scores, -jnp.inf)
            raised = jnp.exp(scores - jnp.max(scores, axis=0, keepdims=True))
            weights_here = raised * (1.0 / jnp.sum(raised, axis=0, keepdims=True))
            heads.append(jnp.dot(value_rows, weights_here.astype(BF16), preferred_element_type=F32))
        joined = heads[0] if len(heads) == 1 else jnp.concatenate(heads, axis=0)
        return joined.T.astype(BF16).reshape(group, tokens, query.shape[1])

    def spread(rz):
        if rz:
            arrived(att_in.at[rz], az_recv.at[rz])
        target = att_buf.at[plane ^ rz, mine]
        for r in range(1, group):
            go(remote(att_in.at[rz, mine ^ r], target, a_send.at[rz, r], a_recv.at[rz, r], within(r)))
        att_buf[plane ^ rz, mine] = att_in[rz, mine]

    for rz in range(wave - 1, 0, -1):
        att_own[rz] = attend(plane ^ rz)
        go(remote(att_own.at[rz], att_in.at[rz], az_send.at[rz], az_recv.at[rz], across(rz)))
        if rz < wave - 2:
            spread(rz + 2)
    att_in[0] = attend(plane)
    for rz in range(min(2, wave - 1), -1, -1):
        spread(rz)
    for rz in range(wave):
        for r in range(1, group):
            arrived(att_buf.at[plane ^ rz, mine ^ r], a_recv.at[rz, r])
    att = jnp.concatenate(
        [att_buf[index // group, index % group] for index in range(wave * group)], axis=1
    )
    stream = (res[...].astype(F32) + att.astype(F32)).astype(BF16).astype(F32)
    inverse = lax.rsqrt(jnp.mean(stream * stream, axis=-1, keepdims=True) + 1e-06)
    normed = (stream * inverse * gain[...]).astype(BF16)
    rows = jnp.dot(chosen.T.astype(BF16), normed, preferred_element_type=F32)
    for expert in range(wave):
        block = rows[expert * capacity:(expert + 1) * capacity]
        outg[expert] = jnp.concatenate([block[:, :half], block[:, half:]], axis=0).astype(BF16)
    for rz in range(1, wave):
        go(remote(outg.at[plane ^ rz], x_buf.at[0, rz], z_send.at[rz], x_recv.at[0, rz], across(rz)))
    x_buf[0, 0] = outg[plane]
    for rz in range(wave):
        if rz:
            arrived(x_buf.at[0, rz], x_recv.at[0, rz])
        for r in (2, 4, 6, 1):
            go(remote(x_buf.at[0, rz], x_buf.at[r, rz], x_send.at[r, rz], x_recv.at[r, rz], within(r)))
    for copy in weights:
        copy.wait()

    def fold(k):
        arrived(core_buf.at[k], c_recv.at[k])
        total = part[2 * k].astype(F32) + core_buf[k].astype(F32)
        sums[k] = total.astype(BF16)
        if k:
            go(remote(sums.at[k], plane_buf.at[k], p_send.at[k], p_recv.at[k], within(2 * k)))

    dims = (((1,), (1,)), ((), ()))
    pairs = group // 2
    for k in range(pairs):
        r = 2 * k
        if k:
            for rz in range(wave):
                arrived(x_buf.at[r, rz], x_recv.at[r, rz])
                go(remote(x_buf.at[r, rz], x_buf.at[r + 1, rz], x_send.at[r + 1, rz],
                          x_recv.at[r + 1, rz], within(1)))
        for rz in range(wave):
            arrived(x_buf.at[r + 1, rz], x_recv.at[r + 1, rz])
        x = x_buf[r:r + 2].reshape(2 * wave * 2 * capacity, half)
        left = lax.dot_general(x, wgu_v[:, :half], dims, preferred_element_type=F32)
        right = lax.dot_general(x, wgu_v[:, half:], dims, preferred_element_type=F32)
        left = left.reshape(2 * wave, 2 * capacity, 2 * hidden_here)[:, :capacity]
        right = right.reshape(2 * wave, 2 * capacity, 2 * hidden_here)[:, capacity:]
        pre = (left + right).reshape(2 * wave * capacity, 2 * hidden_here)
        gate_pre, up_pre = pre[:, :hidden_here], pre[:, hidden_here:]
        hidden = (gate_pre / (1.0 + jnp.exp(-gate_pre)) * up_pre).astype(BF16)
        piece = jnp.dot(hidden, wd_v[...], preferred_element_type=F32).astype(BF16)
        part[r] = piece[:wave * capacity]
        part[r + 1] = piece[wave * capacity:]
        go(remote(part.at[r + 1], core_buf.at[k], c_send.at[k], c_recv.at[k], within(1)))
        if k:
            fold(k - 1)
    fold(pairs - 1)

    total = sums[0].astype(F32)
    for k in range(1, pairs):
        arrived(plane_buf.at[k], p_recv.at[k])
        total = total + plane_buf[k].astype(F32)
    for rz in range(wave):
        block = total[rz * capacity:(rz + 1) * capacity]
        block = jnp.concatenate([block[:, :half], block[:, half:]], axis=0).astype(BF16)
        if rz:
            final[rz] = block
            go(remote(final.at[rz], back.at[plane], b_send.at[rz], b_recv.at[rz], across(rz)))
        else:
            back[plane] = block
    for rz in range(1, wave):
        arrived(back.at[plane ^ rz], b_recv.at[rz])

    high = mix.astype(BF16)
    rest = mix - high.astype(F32)
    middle = rest.astype(BF16)
    low = (rest - middle.astype(F32)).astype(BF16)
    outs = back[...].astype(F32)
    for side in range(2):
        columns = slice(side * half, (side + 1) * half)
        block = outs[:, side * capacity:(side + 1) * capacity].reshape(wave * capacity, half).astype(BF16)
        added = (
            jnp.dot(low, block, preferred_element_type=F32)
            + jnp.dot(middle, block, preferred_element_type=F32)
            + jnp.dot(high, block, preferred_element_type=F32)
        )
        out[:, columns] = (stream[:, columns] + added).astype(BF16)
    for copy in sends:
        copy.wait_send()


def layer(queries, keys, values, span_ids, res, gain, routes, gates, wg, wu, wd):
    devices = lax.axis_size("expert")
    group = FF_WIN // wg.shape[0]
    wave = devices // group
    tokens, width = res.shape
    capacity = tokens // 4
    half = width // 2
    pairs = group // 2
    vmem = pl.BlockSpec(memory_space=pltpu.VMEM)
    hbm = pl.BlockSpec(memory_space=pl.ANY)
    dma = pltpu.SemaphoreType.DMA
    rows = wave * capacity
    return pl.pallas_call(
        functools.partial(moe_kernel, group),
        out_shape=jax.ShapeDtypeStruct((tokens, width), BF16),
        in_specs=[vmem] * 8 + [hbm] * 3,
        out_specs=vmem,
        scratch_shapes=[
            pltpu.VMEM((wave, tokens, 2 * HEAD_DIM), BF16),
            pltpu.VMEM((wave, group, tokens, 2 * HEAD_DIM), BF16),
            pltpu.VMEM((wave, group * tokens, 128), F32),
            pltpu.VMEM((wave, group, tokens, queries.shape[1]), BF16),
            pltpu.VMEM((wave, group, tokens, queries.shape[1]), BF16),
            pltpu.VMEM((wave, group, tokens, queries.shape[1]), BF16),
            dma((wave,)), dma((wave, group)), dma((wave, group)),
            dma((wave,)), dma((wave,)), dma((wave, group)), dma((wave, group)),
            pltpu.VMEM((2 * wg.shape[0], width), BF16),
            pltpu.VMEM((wd.shape[0], width), BF16),
            pltpu.VMEM((wave, 2 * capacity, half), BF16),
            pltpu.VMEM((group, wave, 2 * capacity, half), BF16),
            pltpu.VMEM((group, rows, width), BF16),
            pltpu.VMEM((pairs, rows, width), BF16),
            pltpu.VMEM((pairs, rows, width), BF16),
            pltpu.VMEM((pairs, rows, width), BF16),
            pltpu.VMEM((wave, 2 * capacity, half), BF16),
            pltpu.VMEM((wave, 2 * capacity, half), BF16),
            dma((3,)), dma((wave,)), dma((group, wave)), dma((group, wave)),
            dma((pairs,)), dma((pairs,)), dma((pairs,)), dma((pairs,)), dma((wave,)), dma((wave,)),
        ],
        compiler_params=pltpu.CompilerParams(
            collective_id=0, has_side_effects=True, vmem_limit_bytes=48 * 2**20
        ),
    )(queries, keys, values, span_ids.reshape(wave, 1, group * tokens), res, gain.reshape(1, width), routes, gates, wg, wu, wd)


def solution(mesh):
    return jax.shard_map(
        layer,
        mesh=mesh,
        in_specs=(
            P("dp", "expert"),
            P(("dp", "expert"), None),
            P(("dp", "expert"), None),
            P("dp"),
            P(("dp", "expert"), None),
            P(),
            P(("dp", "expert"), None),
            P(("dp", "expert"), None),
            P("expert", None),
            P("expert", None),
            P("expert", None),
        ),
        out_specs=P(("dp", "expert"), None),
        check_vma=False,
    )
```

```python
import functools
import math

import jax
import jax.numpy as jnp
from jax import lax
from jax.experimental import pallas as pl
from jax.experimental.pallas import tpu as pltpu
from jax.sharding import PartitionSpec as P

KV_HEADS = 4
HEAD_DIM = 64
FF_WIN = 1024
SPAN = 512
MESH = pl.DeviceIdType.MESH
F32 = jnp.float32
BF16 = jnp.bfloat16


def remote(src, dst, send, recv, device):
    return pltpu.make_async_remote_copy(
        src_ref=src, dst_ref=dst, send_sem=send, recv_sem=recv,
        device_id={"expert": device}, device_id_type=MESH,
    )


def route_matrix(routes, gates, wave, capacity):
    tokens = routes.shape[0]
    columns = wave * capacity
    column = lax.broadcasted_iota(jnp.int32, (tokens, columns), 1)
    lower = (
        lax.broadcasted_iota(jnp.int32, (tokens, tokens), 0)
        >= lax.broadcasted_iota(jnp.int32, (tokens, tokens), 1)
    ).astype(F32)
    named_wide = jnp.zeros((tokens, columns), F32)
    weight_wide = jnp.zeros((tokens, columns), F32)
    for expert in range(wave):
        hits = routes == expert
        named = jnp.max(jnp.where(hits, 1.0, 0.0), axis=1, keepdims=True)
        weight = jnp.sum(jnp.where(hits, gates, 0.0), axis=1, keepdims=True)
        here = column // capacity == expert
        named_wide = jnp.where(here, named, named_wide)
        weight_wide = jnp.where(here, weight, weight_wide)
    count = jnp.dot(lower.astype(BF16), named_wide.astype(BF16), preferred_element_type=F32)
    slot = (column % capacity + 1).astype(F32)
    chosen = jnp.where(count == slot, named_wide, 0.0)
    return chosen, chosen * weight_wide


def moe_kernel(
    group, queries_hbm, keys_hbm, values_hbm, ids_hbm, res_hbm, gain_hbm, routes_hbm, gates_hbm, wg, wu, wd, out,
    queries, keys, values, ids, res, gain, routes, gates, in_sem,
    kv_out, kv_buf, id_rows, att_in, att_own, att_buf,
    kz_send, kv_send, kv_recv, az_send, az_recv, a_send, a_recv,
    wgu_v, wd_v, outg, x_buf, part, core_buf, sums, plane_buf, final, back,
    w_sem, z_send, x_send, x_recv, c_send, c_recv, p_send, p_recv, b_send, b_recv,
):
    me = lax.axis_index("expert")
    wave = outg.shape[0]
    capacity = outg.shape[1] // 2
    tokens, width = out.shape
    half = width // 2
    hidden_here = wg.shape[0]
    mine = me % group
    plane = me // group
    base = plane * group

    def across(rz):
        return (plane ^ rz) * group + mine

    def within(r):
        return base + (mine ^ r)

    fetched = {}
    for number, (name, source, target) in enumerate((
        ("keys", keys_hbm, keys), ("values", values_hbm, values), ("ids", ids_hbm, ids),
        ("routes", routes_hbm, routes), ("gates", gates_hbm, gates), ("queries", queries_hbm, queries),
        ("res", res_hbm, res), ("gain", gain_hbm, gain),
    )):
        fetched[name] = pltpu.make_async_copy(source, target, in_sem.at[number])
    weights = [
        pltpu.make_async_copy(wg, wgu_v.at[pl.ds(0, hidden_here)], w_sem.at[0]),
        pltpu.make_async_copy(wu, wgu_v.at[pl.ds(hidden_here, hidden_here)], w_sem.at[1]),
        pltpu.make_async_copy(wd, wd_v, w_sem.at[2]),
    ]
    barrier = pltpu.get_barrier_semaphore()
    partners = [across(rz) for rz in range(1, wave)] + [within(r) for r in range(1, group)]
    for device in partners:
        pl.semaphore_signal(barrier, inc=1, device_id={"expert": device}, device_id_type=MESH)

    for copy in list(fetched.values()) + weights:
        copy.start()
    for name in ("keys", "values"):
        fetched[name].wait()
    for plane_to in range(wave):
        head = plane_to * KV_HEADS // wave
        columns = slice(head * HEAD_DIM, (head + 1) * HEAD_DIM)
        kv_out[plane_to] = jnp.concatenate([keys[:, columns], values[:, columns]], axis=1)
    pl.semaphore_wait(barrier, len(partners))

    sends = []

    def go(copy):
        copy.start()
        sends.append(copy)
        return copy

    def arrived(ref, sem):
        pltpu.make_async_copy(ref, ref, sem).wait()

    for rz in range(1, wave):
        go(remote(kv_out.at[plane ^ rz], kv_buf.at[plane, mine], kz_send.at[rz], kv_recv.at[rz, 0], across(rz)))
    kv_buf[plane, mine] = kv_out[plane]
    for rz in range(wave):
        block = kv_buf.at[plane ^ rz, mine]
        if rz:
            arrived(block, kv_recv.at[rz, 0])
    for r in range(1, group):
        block = kv_buf.at[:, mine]
        go(remote(block, block, kv_send.at[0, r], kv_recv.at[0, r], within(r)))

    for name in ("ids", "routes", "gates", "queries"):
        fetched[name].wait()
    chosen, mix = route_matrix(routes[...].astype(F32).T, gates[...].T, wave, capacity)
    chunk = group * tokens
    for index in range(wave):
        id_rows[index] = jnp.broadcast_to(ids[index].astype(F32), (128, chunk)).T
    for r in range(1, group):
        arrived(kv_buf.at[:, mine ^ r], kv_recv.at[0, r])

    def attend(index):
        planes = SPAN // chunk
        first = index // planes * planes
        block = kv_buf[pl.ds(first, planes)].reshape(SPAN, 2 * HEAD_DIM)
        key_blk = block[:, :HEAD_DIM]
        value_rows = block.T[HEAD_DIM:]
        key_ids = id_rows[pl.ds(first, planes)].reshape(SPAN, 128)
        key_ids = jnp.concatenate([key_ids] * (chunk // 128), axis=1)
        offset = (index - first) * chunk
        ahead = (
            lax.broadcasted_iota(jnp.int32, (SPAN, chunk), 0)
            - lax.broadcasted_iota(jnp.int32, (SPAN, chunk), 1)
        )
        allowed = (ahead <= offset) & (key_ids == ids[index].astype(F32))
        query = queries[pl.ds(pl.multiple_of(index * chunk, chunk), chunk), :] * BF16(1.0 / math.sqrt(HEAD_DIM))
        heads = []
        for head in range(query.shape[1] // HEAD_DIM):
            one = query[:, head * HEAD_DIM:(head + 1) * HEAD_DIM]
            scores = lax.dot_general(key_blk, one, (((1,), (1,)), ((), ())), preferred_element_type=F32)
            scores = jnp.where(allowed, scores, -jnp.inf)
            raised = jnp.exp(scores - jnp.max(scores, axis=0, keepdims=True))
            weights_here = raised * (1.0 / jnp.sum(raised, axis=0, keepdims=True))
            heads.append(jnp.dot(value_rows, weights_here.astype(BF16), preferred_element_type=F32))
        joined = heads[0] if len(heads) == 1 else jnp.concatenate(heads, axis=0)
        return joined.T.astype(BF16).reshape(group, tokens, query.shape[1])

    def spread(rz):
        if rz:
            arrived(att_in.at[rz], az_recv.at[rz])
        target = att_buf.at[plane ^ rz, mine]
        for r in range(1, group):
            go(remote(att_in.at[rz, mine ^ r], target, a_send.at[rz, r], a_recv.at[rz, r], within(r)))
        att_buf[plane ^ rz, mine] = att_in[rz, mine]

    for rz in range(wave - 1, 0, -1):
        att_own[rz] = attend(plane ^ rz)
        go(remote(att_own.at[rz], att_in.at[rz], az_send.at[rz], az_recv.at[rz], across(rz)))
        if rz < wave - 2:
            spread(rz + 2)
    att_in[0] = attend(plane)
    for rz in range(min(2, wave - 1), -1, -1):
        spread(rz)
    for rz in range(wave):
        for r in range(1, group):
            arrived(att_buf.at[plane ^ rz, mine ^ r], a_recv.at[rz, r])
    att = jnp.concatenate(
        [att_buf[index // group, index % group] for index in range(wave * group)], axis=1
    )
    for name in ("res", "gain"):
        fetched[name].wait()
    stream = (res[...].astype(F32) + att.astype(F32)).astype(BF16).astype(F32)
    inverse = lax.rsqrt(jnp.mean(stream * stream, axis=-1, keepdims=True) + 1e-06)
    normed = (stream * inverse * gain[...]).astype(BF16)
    rows = jnp.dot(chosen.T.astype(BF16), normed, preferred_element_type=F32)
    for expert in range(wave):
        block = rows[expert * capacity:(expert + 1) * capacity]
        outg[expert] = jnp.concatenate([block[:, :half], block[:, half:]], axis=0).astype(BF16)
    for rz in range(1, wave):
        go(remote(outg.at[plane ^ rz], x_buf.at[0, rz], z_send.at[rz], x_recv.at[0, rz], across(rz)))
    x_buf[0, 0] = outg[plane]
    for rz in range(wave):
        if rz:
            arrived(x_buf.at[0, rz], x_recv.at[0, rz])
        for r in (2, 4, 1):
            go(remote(x_buf.at[0, rz], x_buf.at[r, rz], x_send.at[r, rz], x_recv.at[r, rz], within(r)))
    for copy in weights:
        copy.wait()

    def fold(k):
        arrived(core_buf.at[k], c_recv.at[k])
        total = part[2 * k].astype(F32) + core_buf[k].astype(F32)
        sums[k] = total.astype(BF16)
        if k:
            go(remote(sums.at[k], plane_buf.at[k], p_send.at[k], p_recv.at[k], within(2 * k)))

    def landed(r, rz):
        arrived(x_buf.at[r, rz], x_recv.at[r, rz])
        go(remote(x_buf.at[r, rz], x_buf.at[r + 1, rz], x_send.at[r + 1, rz], x_recv.at[r + 1, rz], within(1)))

    dims = (((1,), (1,)), ((), ()))
    pairs = group // 2
    for k in range(pairs):
        r = 2 * k
        if k == 1:
            for rz in range(wave):
                for near, other in ((2, 4), (4, 2)):
                    landed(near, rz)
                    if (rz < wave // 2) == (near == 4):
                        go(remote(x_buf.at[near, rz], x_buf.at[6, rz], x_send.at[6, rz],
                                  x_recv.at[6, rz], within(other)))
        if k == 3:
            for rz in range(wave):
                landed(6, rz)
        for rz in range(wave):
            arrived(x_buf.at[r + 1, rz], x_recv.at[r + 1, rz])
        x = x_buf[r:r + 2].reshape(2 * wave * 2 * capacity, half)
        left = lax.dot_general(x, wgu_v[:, :half], dims, preferred_element_type=F32)
        right = lax.dot_general(x, wgu_v[:, half:], dims, preferred_element_type=F32)
        left = left.reshape(2 * wave, 2 * capacity, 2 * hidden_here)[:, :capacity]
        right = right.reshape(2 * wave, 2 * capacity, 2 * hidden_here)[:, capacity:]
        pre = (left + right).reshape(2 * wave * capacity, 2 * hidden_here)
        gate_pre, up_pre = pre[:, :hidden_here], pre[:, hidden_here:]
        hidden = (gate_pre / (1.0 + jnp.exp(-gate_pre)) * up_pre).astype(BF16)
        piece = jnp.dot(hidden, wd_v[...], preferred_element_type=F32).astype(BF16)
        part[r] = piece[:wave * capacity]
        part[r + 1] = piece[wave * capacity:]
        go(remote(part.at[r + 1], core_buf.at[k], c_send.at[k], c_recv.at[k], within(1)))
        if k:
            fold(k - 1)
    fold(pairs - 1)

    total = sums[0].astype(F32)
    for k in range(1, pairs):
        arrived(plane_buf.at[k], p_recv.at[k])
        total = total + plane_buf[k].astype(F32)
    for rz in range(wave):
        block = total[rz * capacity:(rz + 1) * capacity]
        block = jnp.concatenate([block[:, :half], block[:, half:]], axis=0).astype(BF16)
        if rz:
            final[rz] = block
            go(remote(final.at[rz], back.at[plane], b_send.at[rz], b_recv.at[rz], across(rz)))
        else:
            back[plane] = block
    for rz in range(1, wave):
        arrived(back.at[plane ^ rz], b_recv.at[rz])

    high = mix.astype(BF16)
    rest = mix - high.astype(F32)
    middle = rest.astype(BF16)
    low = (rest - middle.astype(F32)).astype(BF16)
    outs = back[...].astype(F32)
    for side in range(2):
        columns = slice(side * half, (side + 1) * half)
        block = outs[:, side * capacity:(side + 1) * capacity].reshape(wave * capacity, half).astype(BF16)
        added = (
            jnp.dot(low, block, preferred_element_type=F32)
            + jnp.dot(middle, block, preferred_element_type=F32)
            + jnp.dot(high, block, preferred_element_type=F32)
        )
        out[:, columns] = (stream[:, columns] + added).astype(BF16)
    for copy in sends:
        copy.wait_send()


def layer(queries, keys, values, span_ids, res, gain, routes, gates, wg, wu, wd):
    devices = lax.axis_size("expert")
    group = FF_WIN // wg.shape[0]
    wave = devices // group
    tokens, width = res.shape
    capacity = tokens // 4
    half = width // 2
    pairs = group // 2
    vmem = pl.BlockSpec(memory_space=pltpu.VMEM)
    hbm = pl.BlockSpec(memory_space=pl.ANY)
    dma = pltpu.SemaphoreType.DMA
    rows = wave * capacity
    return pl.pallas_call(
        functools.partial(moe_kernel, group),
        out_shape=jax.ShapeDtypeStruct((tokens, width), BF16),
        in_specs=[hbm] * 11,
        out_specs=vmem,
        scratch_shapes=[
            pltpu.VMEM(queries.shape, BF16),
            pltpu.VMEM(keys.shape, BF16),
            pltpu.VMEM(values.shape, BF16),
            pltpu.VMEM((wave, 1, group * tokens), jnp.int32),
            pltpu.VMEM(res.shape, BF16),
            pltpu.VMEM((1, width), F32),
            pltpu.VMEM(routes.shape[::-1], jnp.int32),
            pltpu.VMEM(gates.shape[::-1], F32),
            dma((8,)),
            pltpu.VMEM((wave, tokens, 2 * HEAD_DIM), BF16),
            pltpu.VMEM((wave, group, tokens, 2 * HEAD_DIM), BF16),
            pltpu.VMEM((wave, group * tokens, 128), F32),
            pltpu.VMEM((wave, group, tokens, queries.shape[1]), BF16),
            pltpu.VMEM((wave, group, tokens, queries.shape[1]), BF16),
            pltpu.VMEM((wave, group, tokens, queries.shape[1]), BF16),
            dma((wave,)), dma((wave, group)), dma((wave, group)),
            dma((wave,)), dma((wave,)), dma((wave, group)), dma((wave, group)),
            pltpu.VMEM((2 * wg.shape[0], width), BF16),
            pltpu.VMEM((wd.shape[0], width), BF16),
            pltpu.VMEM((wave, 2 * capacity, half), BF16),
            pltpu.VMEM((group, wave, 2 * capacity, half), BF16),
            pltpu.VMEM((group, rows, width), BF16),
            pltpu.VMEM((pairs, rows, width), BF16),
            pltpu.VMEM((pairs, rows, width), BF16),
            pltpu.VMEM((pairs, rows, width), BF16),
            pltpu.VMEM((wave, 2 * capacity, half), BF16),
            pltpu.VMEM((wave, 2 * capacity, half), BF16),
            dma((3,)), dma((wave,)), dma((group, wave)), dma((group, wave)),
            dma((pairs,)), dma((pairs,)), dma((pairs,)), dma((pairs,)), dma((wave,)), dma((wave,)),
        ],
        compiler_params=pltpu.CompilerParams(
            collective_id=0, has_side_effects=True, vmem_limit_bytes=60 * 2**20
        ),
    )(queries, keys, values, span_ids.reshape(wave, 1, group * tokens), res, gain.reshape(1, width), routes.T, gates.T, wg, wu, wd)


def solution(mesh):
    return jax.shard_map(
        layer,
        mesh=mesh,
        in_specs=(
            P("dp", "expert"),
            P(("dp", "expert"), None),
            P(("dp", "expert"), None),
            P("dp"),
            P(("dp", "expert"), None),
            P(),
            P(("dp", "expert"), None),
            P(("dp", "expert"), None),
            P("expert", None),
            P("expert", None),
            P("expert", None),
        ),
        out_specs=P(("dp", "expert"), None),
        check_vma=False,
    )
```

```python
import functools
import math

import jax
import jax.numpy as jnp
from jax import lax
from jax.experimental import pallas as pl
from jax.experimental.pallas import tpu as pltpu
from jax.sharding import PartitionSpec as P

KV_HEADS = 4
HEAD_DIM = 64
FF_WIN = 1024
SPAN = 512
MESH = pl.DeviceIdType.MESH
F32 = jnp.float32
BF16 = jnp.bfloat16


def remote(src, dst, send, recv, device):
    return pltpu.make_async_remote_copy(
        src_ref=src, dst_ref=dst, send_sem=send, recv_sem=recv,
        device_id={"expert": device}, device_id_type=MESH,
    )


def route_matrix(routes, gates, wave, capacity):
    tokens = routes.shape[0]
    columns = wave * capacity
    column = lax.broadcasted_iota(jnp.int32, (tokens, columns), 1)
    lower = (
        lax.broadcasted_iota(jnp.int32, (tokens, tokens), 0)
        >= lax.broadcasted_iota(jnp.int32, (tokens, tokens), 1)
    ).astype(F32)
    named_wide = jnp.zeros((tokens, columns), F32)
    weight_wide = jnp.zeros((tokens, columns), F32)
    for expert in range(wave):
        hits = routes == expert
        named = jnp.max(jnp.where(hits, 1.0, 0.0), axis=1, keepdims=True)
        weight = jnp.sum(jnp.where(hits, gates, 0.0), axis=1, keepdims=True)
        here = column // capacity == expert
        named_wide = jnp.where(here, named, named_wide)
        weight_wide = jnp.where(here, weight, weight_wide)
    count = jnp.dot(lower.astype(BF16), named_wide.astype(BF16), preferred_element_type=F32)
    slot = (column % capacity + 1).astype(F32)
    chosen = jnp.where(count == slot, named_wide, 0.0)
    return chosen, chosen * weight_wide


def moe_kernel(
    group, queries_hbm, keys_hbm, values_hbm, ids_hbm, res_hbm, gain_hbm, routes_hbm, gates_hbm, wg, wu, wd, out,
    queries, keys, values, ids, res, gain, routes, gates, in_sem,
    kv_out, kv_buf, id_rows, att_in, att_own, att_buf,
    kz_send, kv_send, kv_recv, az_send, az_recv, a_send, a_recv,
    wgu_v, wd_v, outg, x_buf, part, core_buf, sums, plane_buf, final, back,
    w_sem, z_send, x_send, x_recv, c_send, c_recv, p_send, p_recv, b_send, b_recv,
):
    me = lax.axis_index("expert")
    wave = outg.shape[0]
    capacity = outg.shape[1] // 2
    tokens, width = out.shape
    half = width // 2
    hidden_here = wg.shape[0]
    mine = me % group
    plane = me // group
    base = plane * group

    def across(rz):
        return (plane ^ rz) * group + mine

    def within(r):
        return base + (mine ^ r)

    fetched = {}
    for number, (name, source, target) in enumerate((
        ("keys", keys_hbm, keys), ("values", values_hbm, values), ("ids", ids_hbm, ids),
        ("routes", routes_hbm, routes), ("gates", gates_hbm, gates), ("queries", queries_hbm, queries),
        ("res", res_hbm, res), ("gain", gain_hbm, gain),
    )):
        fetched[name] = pltpu.make_async_copy(source, target, in_sem.at[number])
    weights = [
        pltpu.make_async_copy(wg, wgu_v.at[pl.ds(0, hidden_here)], w_sem.at[0]),
        pltpu.make_async_copy(wu, wgu_v.at[pl.ds(hidden_here, hidden_here)], w_sem.at[1]),
        pltpu.make_async_copy(wd, wd_v, w_sem.at[2]),
    ]
    barrier = pltpu.get_barrier_semaphore()
    partners = [across(rz) for rz in range(1, wave)] + [within(r) for r in range(1, group)]
    for device in partners:
        pl.semaphore_signal(barrier, inc=1, device_id={"expert": device}, device_id_type=MESH)

    for copy in list(fetched.values()) + weights:
        copy.start()
    for name in ("keys", "values"):
        fetched[name].wait()
    for plane_to in range(wave):
        head = plane_to * KV_HEADS // wave
        columns = slice(head * HEAD_DIM, (head + 1) * HEAD_DIM)
        kv_out[plane_to] = jnp.concatenate([keys[:, columns], values[:, columns]], axis=1)
    pl.semaphore_wait(barrier, len(partners))

    sends = []

    def go(copy):
        copy.start()
        sends.append(copy)
        return copy

    def arrived(ref, sem):
        pltpu.make_async_copy(ref, ref, sem).wait()

    for rz in range(1, wave):
        go(remote(kv_out.at[plane ^ rz], kv_buf.at[plane, mine], kz_send.at[rz], kv_recv.at[rz, 0], across(rz)))
    kv_buf[plane, mine] = kv_out[plane]
    for rz in range(wave):
        block = kv_buf.at[plane ^ rz, mine]
        if rz:
            arrived(block, kv_recv.at[rz, 0])
    for r in range(1, group):
        block = kv_buf.at[:, mine]
        go(remote(block, block, kv_send.at[0, r], kv_recv.at[0, r], within(r)))

    for name in ("ids", "routes", "gates", "queries"):
        fetched[name].wait()
    chosen, mix = route_matrix(routes[...].astype(F32).T, gates[...].T, wave, capacity)
    chunk = group * tokens
    for index in range(wave):
        id_rows[index] = jnp.broadcast_to(ids[index].astype(F32), (128, chunk)).T
    for r in range(1, group):
        arrived(kv_buf.at[:, mine ^ r], kv_recv.at[0, r])

    def attend(index):
        planes = SPAN // chunk
        first = index // planes * planes
        block = kv_buf[pl.ds(first, planes)].reshape(SPAN, 2 * HEAD_DIM)
        key_blk = block[:, :HEAD_DIM]
        value_rows = block.T[HEAD_DIM:]
        key_ids = id_rows[pl.ds(first, planes)].reshape(SPAN, 128)
        key_ids = jnp.concatenate([key_ids] * (chunk // 128), axis=1)
        offset = (index - first) * chunk
        ahead = (
            lax.broadcasted_iota(jnp.int32, (SPAN, chunk), 0)
            - lax.broadcasted_iota(jnp.int32, (SPAN, chunk), 1)
        )
        allowed = (ahead <= offset) & (key_ids == ids[index].astype(F32))
        query = queries[pl.ds(pl.multiple_of(index * chunk, chunk), chunk), :] * BF16(1.0 / math.sqrt(HEAD_DIM))
        heads = []
        for head in range(query.shape[1] // HEAD_DIM):
            one = query[:, head * HEAD_DIM:(head + 1) * HEAD_DIM]
            scores = lax.dot_general(key_blk, one, (((1,), (1,)), ((), ())), preferred_element_type=F32)
            scores = jnp.where(allowed, scores, -jnp.inf)
            raised = jnp.exp(scores - jnp.max(scores, axis=0, keepdims=True))
            weights_here = raised * (1.0 / jnp.sum(raised, axis=0, keepdims=True))
            heads.append(jnp.dot(value_rows, weights_here.astype(BF16), preferred_element_type=F32))
        joined = heads[0] if len(heads) == 1 else jnp.concatenate(heads, axis=0)
        return joined.T.astype(BF16).reshape(group, tokens, query.shape[1])

    later = wave // 2

    def spread(part_at, first):
        block = pl.ds(first, later)
        for rz in range(first, first + later):
            if rz:
                arrived(att_in.at[rz], az_recv.at[rz])
        for r in range(1, group):
            go(remote(att_in.at[block, mine ^ r], att_buf.at[block, mine],
                      a_send.at[part_at, r], a_recv.at[part_at, r], within(r)))
        att_buf[block, mine] = att_in[block, mine]

    for rz in range(wave - 1, 0, -1):
        att_own[rz] = attend(plane ^ rz)
        go(remote(att_own.at[rz], att_in.at[rz], az_send.at[rz], az_recv.at[rz], across(rz)))
    spread(0, later)
    att_in[0] = attend(plane)
    spread(1, 0)
    for part_at, first in ((0, later), (1, 0)):
        for r in range(1, group):
            arrived(att_buf.at[pl.ds(first, later), mine ^ r], a_recv.at[part_at, r])
    att = jnp.concatenate(
        [att_buf[plane ^ (index // group), index % group] for index in range(wave * group)], axis=1
    )
    for name in ("res", "gain"):
        fetched[name].wait()
    stream = (res[...].astype(F32) + att.astype(F32)).astype(BF16).astype(F32)
    inverse = lax.rsqrt(jnp.mean(stream * stream, axis=-1, keepdims=True) + 1e-06)
    normed = (stream * inverse * gain[...]).astype(BF16)
    rows = jnp.dot(chosen.T.astype(BF16), normed, preferred_element_type=F32)
    for expert in range(wave):
        block = rows[expert * capacity:(expert + 1) * capacity]
        outg[expert] = jnp.concatenate([block[:, :half], block[:, half:]], axis=0).astype(BF16)
    for rz in range(1, wave):
        go(remote(outg.at[plane ^ rz], x_buf.at[0, rz], z_send.at[rz], x_recv.at[0, rz], across(rz)))
    x_buf[0, 0] = outg[plane]
    for rz in range(wave):
        if rz:
            arrived(x_buf.at[0, rz], x_recv.at[0, rz])
        for r in (2, 4, 1):
            go(remote(x_buf.at[0, rz], x_buf.at[r, rz], x_send.at[r, rz], x_recv.at[r, rz], within(r)))
    for copy in weights:
        copy.wait()

    def fold(k):
        arrived(core_buf.at[k], c_recv.at[k])
        for rz in range(wave - 1, -1, -1):
            sums[k, rz] = (part[2 * k, rz].astype(F32) + core_buf[k, rz].astype(F32)).astype(BF16)
            go(remote(sums.at[k, rz], plane_buf.at[k, rz], p_send.at[k, rz], p_recv.at[k, rz], within(2 * k)))

    def landed(r, rz):
        arrived(x_buf.at[r, rz], x_recv.at[r, rz])
        go(remote(x_buf.at[r, rz], x_buf.at[r + 1, rz], x_send.at[r + 1, rz], x_recv.at[r + 1, rz], within(1)))

    dims = (((1,), (1,)), ((), ()))
    pairs = group // 2
    for k in range(pairs):
        r = 2 * k
        if k == 1:
            for rz in range(wave):
                for near, other in ((2, 4), (4, 2)):
                    landed(near, rz)
                    if (rz < wave // 2) == (near == 4):
                        go(remote(x_buf.at[near, rz], x_buf.at[6, rz], x_send.at[6, rz],
                                  x_recv.at[6, rz], within(other)))
        if k == 3:
            for rz in range(wave):
                landed(6, rz)
        for rz in range(wave):
            arrived(x_buf.at[r + 1, rz], x_recv.at[r + 1, rz])
        x = x_buf[r:r + 2].reshape(2 * wave * 2 * capacity, half)
        left = lax.dot_general(x, wgu_v[:, :half], dims, preferred_element_type=F32)
        right = lax.dot_general(x, wgu_v[:, half:], dims, preferred_element_type=F32)
        left = left.reshape(2 * wave, 2 * capacity, 2 * hidden_here)[:, :capacity]
        right = right.reshape(2 * wave, 2 * capacity, 2 * hidden_here)[:, capacity:]
        pre = (left + right).reshape(2 * wave * capacity, 2 * hidden_here)
        gate_pre, up_pre = pre[:, :hidden_here], pre[:, hidden_here:]
        hidden = (gate_pre / (1.0 + jnp.exp(-gate_pre)) * up_pre).astype(BF16)
        piece = jnp.dot(hidden, wd_v[...], preferred_element_type=F32)
        for number in range(2 * wave):
            block = piece[number * capacity:(number + 1) * capacity]
            block = jnp.concatenate([block[:, :half], block[:, half:]], axis=0).astype(BF16)
            part[r + number // wave, number % wave] = block
        go(remote(part.at[r + 1], core_buf.at[k], c_send.at[k], c_recv.at[k], within(1)))
        if k > 1:
            fold(k - 1)
    fold(pairs - 1)

    arrived(core_buf.at[0], c_recv.at[0])
    for rz in range(wave - 1, -1, -1):
        total = part[0, rz].astype(F32) + core_buf[0, rz].astype(F32)
        for k in range(1, pairs):
            arrived(plane_buf.at[k, rz], p_recv.at[k, rz])
            total = total + plane_buf[k, rz].astype(F32)
        if rz:
            final[rz] = total.astype(BF16)
            go(remote(final.at[rz], back.at[plane], b_send.at[rz], b_recv.at[rz], across(rz)))
        else:
            back[plane] = total.astype(BF16)
    for rz in range(1, wave):
        arrived(back.at[plane ^ rz], b_recv.at[rz])

    high = mix.astype(BF16)
    rest = mix - high.astype(F32)
    middle = rest.astype(BF16)
    low = (rest - middle.astype(F32)).astype(BF16)
    outs = back[...].astype(F32)
    for side in range(2):
        columns = slice(side * half, (side + 1) * half)
        block = outs[:, side * capacity:(side + 1) * capacity].reshape(wave * capacity, half).astype(BF16)
        added = (
            jnp.dot(low, block, preferred_element_type=F32)
            + jnp.dot(middle, block, preferred_element_type=F32)
            + jnp.dot(high, block, preferred_element_type=F32)
        )
        out[:, columns] = (stream[:, columns] + added).astype(BF16)
    for copy in sends:
        copy.wait_send()


def layer(queries, keys, values, span_ids, res, gain, routes, gates, wg, wu, wd):
    devices = lax.axis_size("expert")
    group = FF_WIN // wg.shape[0]
    wave = devices // group
    tokens, width = res.shape
    capacity = tokens // 4
    half = width // 2
    pairs = group // 2
    vmem = pl.BlockSpec(memory_space=pltpu.VMEM)
    hbm = pl.BlockSpec(memory_space=pl.ANY)
    dma = pltpu.SemaphoreType.DMA
    return pl.pallas_call(
        functools.partial(moe_kernel, group),
        out_shape=jax.ShapeDtypeStruct((tokens, width), BF16),
        in_specs=[hbm] * 11,
        out_specs=vmem,
        scratch_shapes=[
            pltpu.VMEM(queries.shape, BF16),
            pltpu.VMEM(keys.shape, BF16),
            pltpu.VMEM(values.shape, BF16),
            pltpu.VMEM((wave, 1, group * tokens), jnp.int32),
            pltpu.VMEM(res.shape, BF16),
            pltpu.VMEM((1, width), F32),
            pltpu.VMEM(routes.shape[::-1], jnp.int32),
            pltpu.VMEM(gates.shape[::-1], F32),
            dma((8,)),
            pltpu.VMEM((wave, tokens, 2 * HEAD_DIM), BF16),
            pltpu.VMEM((wave, group, tokens, 2 * HEAD_DIM), BF16),
            pltpu.VMEM((wave, group * tokens, 128), F32),
            pltpu.VMEM((wave, group, tokens, queries.shape[1]), BF16),
            pltpu.VMEM((wave, group, tokens, queries.shape[1]), BF16),
            pltpu.VMEM((wave, group, tokens, queries.shape[1]), BF16),
            dma((wave,)), dma((wave, group)), dma((wave, group)),
            dma((wave,)), dma((wave,)), dma((wave, group)), dma((wave, group)),
            pltpu.VMEM((2 * wg.shape[0], width), BF16),
            pltpu.VMEM((wd.shape[0], width), BF16),
            pltpu.VMEM((wave, 2 * capacity, half), BF16),
            pltpu.VMEM((group, wave, 2 * capacity, half), BF16),
            pltpu.VMEM((group, wave, 2 * capacity, half), BF16),
            pltpu.VMEM((pairs, wave, 2 * capacity, half), BF16),
            pltpu.VMEM((pairs, wave, 2 * capacity, half), BF16),
            pltpu.VMEM((pairs, wave, 2 * capacity, half), BF16),
            pltpu.VMEM((wave, 2 * capacity, half), BF16),
            pltpu.VMEM((wave, 2 * capacity, half), BF16),
            dma((3,)), dma((wave,)), dma((group, wave)), dma((group, wave)),
            dma((pairs,)), dma((pairs,)), dma((pairs, wave)), dma((pairs, wave)), dma((wave,)), dma((wave,)),
        ],
        compiler_params=pltpu.CompilerParams(
            collective_id=0, has_side_effects=True, vmem_limit_bytes=60 * 2**20
        ),
    )(queries, keys, values, span_ids.reshape(wave, 1, group * tokens), res, gain.reshape(1, width), routes.T, gates.T, wg, wu, wd)


def solution(mesh):
    return jax.shard_map(
        layer,
        mesh=mesh,
        in_specs=(
            P("dp", "expert"),
            P(("dp", "expert"), None),
            P(("dp", "expert"), None),
            P("dp"),
            P(("dp", "expert"), None),
            P(),
            P(("dp", "expert"), None),
            P(("dp", "expert"), None),
            P("expert", None),
            P("expert", None),
            P("expert", None),
        ),
        out_specs=P(("dp", "expert"), None),
        check_vma=False,
    )
```
